512 devices in a mesh: frow: 16 (over y_hi, x, core), fcol: 32 (over y_lo, z).
Axes of the slice: x: 4, y: 8 (y_hi: 2, y_lo: 4; y = y_hi * 4 + y_lo), z: 8, core: 2. Of those that a mesh axis runs over, the one named last changes fastest.
Arguments:
- state: bfloat16 [12, 256, 256, 256], P(None, 'frow', 'fcol'), may hold values from -6 to 6
- gate_kernel: bfloat16 [3, 3, 256, 128], replicated, may hold values from -0.125 to 0.125
- dilated_kernel: bfloat16 [3, 3, 256, 128], replicated, may hold values from -0.125 to 0.125
- hidden_grad: bfloat16 [12, 256, 256, 128], P(None, 'frow', 'fcol'), may hold values from -6 to 6
- seam_face: int32 [12, 4], replicated, may hold values from 0 to 11
- seam_code: int32 [12, 4], replicated, may hold values from 0 to 3
- corner_mask: int32 [12, 4], replicated, may hold values 0 or 1
Outputs:
- hidden: bfloat16 [12, 256, 256, 128], P(None, 'frow', 'fcol')
- gate_kernel_grad: float32 [294912], P(('frow', 'fcol'))
- dilated_kernel_grad: float32 [294912], P(('frow', 'fcol'))
The draws below stay inside these ranges and needn't reach their ends.
Inputs may be any that keep to these rules, and one draw needn't show every extreme that they name: `seam_face`: faces are numbered 0 to 11. `seam_code`: bit 1 picks the neighbour's side within the pair (north or south, west or east), bit 0 reverses the edge.
All inputs are finite; a program needn't handle non-finite values.
Results may differ from the reference program's by a relative error of at most 0.0029.
Values may be sent and summed in bfloat16 or wider, within the bound.
No kernel may reach another device: no remote copies, remote signals or barrier semaphores. Data moves between devices by JAX's collectives and lax.ppermute only.
A program may use at most 64 MiB of HBM per device.

```python
import jax
import jax.numpy as jnp
from jax import lax

FACES = 12
C_IN = 256
C_OUT = 128
NSIDE = 256


def with_ends(result, own_key, least, largest):
    longest = result.shape.index(max(result.shape))
    spots = []
    for shift in (0, 1):
        where = [jax.random.randint(jax.random.fold_in(own_key, axis), (), 0, length) for axis, length in enumerate(result.shape)]
        where[longest] = (where[longest] + shift) % result.shape[longest]
        spots.append(tuple(where))
    return result.at[spots[0]].set(least).at[spots[1]].set(largest)


def shard_levels(stream_key, shape, pieces, low, top_value):
    factor_of, own = 1.0, jax.random.fold_in(stream_key, 6)
    for dim, shards_of in pieces:
        steps = jnp.exp(jax.random.uniform(jax.random.fold_in(own, dim), (shards_of,), jnp.float32, low / len(pieces), top_value / len(pieces)))
        factor_of = factor_of * jnp.repeat(steps, shape[dim] // shards_of).reshape([-1 if axis == dim else 1 for axis in range(len(shape))])
    return factor_of


def scatter_about(key, dims, scale, bound, split=(), kind=jnp.bfloat16):
    array = jax.random.normal(key, dims, jnp.float32) * scale
    if len(split) > 0:
        array = shard_levels(key, dims, split, -0.22, 0.18) * array
    return jnp.clip(array, min=-bound, max=bound).astype(kind)


def setup_inputs(seed: int = 0) -> dict:
    keys = jax.random.split(jax.random.key(seed), 8)
    state = scatter_about(keys[0], (FACES, NSIDE, NSIDE, C_IN), 1.0, 6.0, ((1, 16), (2, 32)))
    gate_kernel = scatter_about(keys[1], (3, 3, C_IN, C_OUT), (9 * C_IN) ** -0.5, 0.125)
    dilated_kernel = scatter_about(keys[2], (3, 3, C_IN, C_OUT), (9 * C_IN) ** -0.5, 0.125)
    hidden_grad = scatter_about(keys[3], (FACES, NSIDE, NSIDE, C_OUT), 1.0, 6.0, ((1, 16), (2, 32)))
    seam_face = with_ends(jax.random.randint(keys[4], (FACES, 4), 0, FACES), jax.random.fold_in(keys[4], 1), 0, FACES - 1).astype(jnp.int32)
    seam_code = with_ends(jax.random.randint(keys[5], (FACES, 4), 0, 4), jax.random.fold_in(keys[5], 1), 0, 3).astype(jnp.int32)
    corner_mask = with_ends((jax.random.randint(keys[6], (FACES, 4), 0, 2) < 1).astype(jnp.int32), jax.random.fold_in(keys[6], 1), 0, 1)
    return dict(state=state, gate_kernel=gate_kernel, dilated_kernel=dilated_kernel, hidden_grad=hidden_grad, seam_face=seam_face, seam_code=seam_code, corner_mask=corner_mask)


def pad_pass(faces, seam_face, seam_code):
    count = faces.shape[0]
    north_side = faces[:, :2]
    south_side = jnp.flip(faces, 1)[:, :2]
    candidates = jnp.stack([north_side, jnp.flip(north_side, 2), south_side, jnp.flip(south_side, 2)])
    candidates = candidates.reshape((4 * count,) + north_side.shape[1:])
    upper_rows = jnp.take(candidates, seam_code[:, 0] * count + seam_face[:, 0], axis=0)
    lower_rows = jnp.take(candidates, seam_code[:, 1] * count + seam_face[:, 1], axis=0)
    return jnp.concatenate([jnp.flip(upper_rows, 1), faces, lower_rows], axis=1)

def corner_factor(upper, lower, left, right, corner_mask):
    weights = corner_mask.astype(jnp.float32) - 1.0
    factor = 1.0 + weights[:, 0, None, None] * upper[None, :, None] * left[None, None, :]
    factor = factor + weights[:, 1, None, None] * upper[None, :, None] * right[None, None, :]
    factor = factor + weights[:, 2, None, None] * lower[None, :, None] * left[None, None, :]
    factor = factor + weights[:, 3, None, None] * lower[None, :, None] * right[None, None, :]
    return factor

def kernel_grad(padded, delta, spacing):
    height = delta.shape[1]
    width = delta.shape[2]
    flat_delta = delta.reshape(-1, delta.shape[-1])
    taps = []
    for tap_row in range(3):
        for tap_col in range(3):
            window = padded[:, tap_row * spacing:tap_row * spacing + height, tap_col * spacing:tap_col * spacing + width]
            window = window.reshape(-1, padded.shape[-1])
            taps.append(lax.dot_general(window, flat_delta, (((0,), (0,)), ((), ())), preferred_element_type=jnp.float32))
    return jnp.stack(taps)

def reference(state, gate_kernel, dilated_kernel, hidden_grad, seam_face, seam_code, corner_mask):
    rows_padded = pad_pass(state, seam_face[:, 0:2], seam_code[:, 0:2])
    turned = jnp.transpose(rows_padded, (0, 2, 1, 3))
    padded = jnp.transpose(pad_pass(turned, seam_face[:, 2:4], seam_code[:, 2:4]), (0, 2, 1, 3))
    extent = padded.shape[1]
    places = jnp.arange(extent)
    low_band = (places < 2).astype(jnp.float32)
    high_band = (places >= extent - 2).astype(jnp.float32)
    factor = corner_factor(low_band, high_band, low_band, high_band, corner_mask)
    padded = padded * factor.astype(padded.dtype)[..., None]
    numbers = ('NHWC', 'HWIO', 'NHWC')
    inner = padded[:, 1:-1, 1:-1]
    gate_pre = lax.conv_general_dilated(inner, gate_kernel, (1, 1), 'VALID', dimension_numbers=numbers, preferred_element_type=jnp.float32)
    value_pre = lax.conv_general_dilated(padded, dilated_kernel, (1, 1), 'VALID', rhs_dilation=(2, 2), dimension_numbers=numbers, preferred_element_type=jnp.float32)
    activated, pullback = jax.vjp(jax.nn.gelu, gate_pre)
    hidden = (activated * value_pre).astype(jnp.bfloat16)
    upstream = hidden_grad.astype(jnp.float32)
    gate_delta = pullback(upstream * value_pre)[0].astype(jnp.bfloat16)
    value_delta = (upstream * activated).astype(jnp.bfloat16)
    scale = (FACES * NSIDE * NSIDE) ** (-0.5)
    gate_grad = (kernel_grad(inner, gate_delta, 1) * scale).reshape(-1)
    dilated_grad = (kernel_grad(padded, value_delta, 2) * scale).reshape(-1)
    return (hidden, gate_grad, dilated_grad)
```

```python
import jax
import jax.numpy as jnp
from jax import lax
from jax.sharding import Mesh
from jax.sharding import PartitionSpec as P

ROWS = ("yh", "x", "c")
COLS = ("yl", "z")


def on_device(state, gate_kernel, dilated_kernel, hidden_grad, seam_face, seam_code, corner_mask):
    count, height, width, _ = state.shape
    n_row = lax.axis_size(ROWS)
    n_col = lax.axis_size(COLS)
    row_index = lax.axis_index(ROWS)
    col_index = lax.axis_index(COLS)
    row_last = n_row - 1
    col_last = n_col - 1
    everywhere = ROWS + COLS

    def place(i, j):
        return i * n_col + j

    def edge_index(side):
        return seam_code[:, side] * count + seam_face[:, side]

    north = state[:, :2]
    south = state[:, height - 2 :]
    own_edge = jnp.where(row_index == 0, north, jnp.flip(south, 1))
    from_above = lax.ppermute(south, ROWS, [(i, (i + 1) % n_row) for i in range(n_row)])
    from_below = lax.ppermute(north, ROWS, [((i + 1) % n_row, i) for i in range(n_row)])
    same = [(place(i, j), place(i, col_last - j)) for i in (0, row_last) for j in range(n_col)]
    other = [
        (place(i, j), place(row_last - i, col_last - j)) for i in (0, row_last) for j in range(n_col)
    ]
    mirror_same = jnp.flip(lax.ppermute(own_edge, everywhere, same), 2)
    mirror_other = jnp.flip(lax.ppermute(own_edge, everywhere, other), 2)
    first = row_index == 0
    far_edge = jnp.where(first, jnp.flip(from_above, 1), from_below)
    candidates = jnp.stack(
        [
            jnp.where(first, own_edge, far_edge),
            jnp.where(first, mirror_same, mirror_other),
            jnp.where(first, far_edge, own_edge),
            jnp.where(first, mirror_other, mirror_same),
        ]
    ).reshape((4 * count,) + north.shape[1:])
    picked = jnp.take(candidates, jnp.where(first, edge_index(0), edge_index(1)), axis=0)
    upper = jnp.where(first, jnp.flip(picked, 1), from_above)
    lower = jnp.where(row_index == row_last, picked, from_below)
    rows_padded = jnp.concatenate([upper, state, lower], axis=1)

    west = rows_padded[:, :, :2]
    east = rows_padded[:, :, width - 2 :]
    first = col_index == 0
    own_edge = jnp.where(first, west, jnp.flip(east, 2))
    from_left = lax.ppermute(east, COLS, [(i, (i + 1) % n_col) for i in range(n_col)])
    from_right = lax.ppermute(west, COLS, [((i + 1) % n_col, i) for i in range(n_col)])
    same = [(place(i, j), place(row_last - i, j)) for i in range(n_row) for j in (0, col_last)]
    other = [
        (place(i, j), place(row_last - i, col_last - j)) for i in range(n_row) for j in (0, col_last)
    ]
    mirror_same = jnp.flip(lax.ppermute(own_edge, everywhere, same), 1)
    mirror_other = jnp.flip(lax.ppermute(own_edge, everywhere, other), 1)
    far_edge = jnp.where(first, jnp.flip(from_left, 2), from_right)
    candidates = jnp.stack(
        [
            jnp.where(first, own_edge, far_edge),
            jnp.where(first, mirror_same, mirror_other),
            jnp.where(first, far_edge, own_edge),
            jnp.where(first, mirror_other, mirror_same),
        ]
    ).reshape((4 * count,) + west.shape[1:])
    picked = jnp.take(candidates, jnp.where(first, edge_index(2), edge_index(3)), axis=0)
    left = jnp.where(first, jnp.flip(picked, 2), from_left)
    right = jnp.where(col_index == col_last, picked, from_right)

    spots = jnp.arange(height + 4)
    top = ((spots < 2) & (row_index == 0))[None, :]
    bottom = ((spots >= height + 2) & (row_index == row_last))[None, :]

    def masked(cols, here, north_mask, south_mask):
        gone = (top & (north_mask == 0)[:, None]) | (bottom & (south_mask == 0)[:, None])
        return jnp.where((gone & here)[:, :, None, None], 0, cols)

    left = masked(left, col_index == 0, corner_mask[:, 0], corner_mask[:, 2])
    right = masked(right, col_index == col_last, corner_mask[:, 1], corner_mask[:, 3])
    padded = jnp.concatenate([left, rows_padded, right], axis=2)

    numbers = ("NHWC", "HWIO", "NHWC")
    inner = padded[:, 1:-1, 1:-1]
    gate_pre = lax.conv_general_dilated(
        inner, gate_kernel, (1, 1), "VALID", dimension_numbers=numbers, preferred_element_type=jnp.float32
    )
    value_pre = lax.conv_general_dilated(
        padded,
        dilated_kernel,
        (1, 1),
        "VALID",
        rhs_dilation=(2, 2),
        dimension_numbers=numbers,
        preferred_element_type=jnp.float32,
    )
    activated, pullback = jax.vjp(jax.nn.gelu, gate_pre)
    hidden = (activated * value_pre).astype(jnp.bfloat16)
    upstream = hidden_grad.astype(jnp.float32)
    gate_delta = pullback(upstream * value_pre)[0].astype(jnp.bfloat16)
    value_delta = (upstream * activated).astype(jnp.bfloat16)

    terms = []
    for windows, delta, spacing in ((inner, gate_delta, 1), (padded, value_delta, 2)):
        flat_delta = delta.reshape(-1, delta.shape[-1])
        for a in range(3):
            for b in range(3):
                window = windows[:, a * spacing : a * spacing + height, b * spacing : b * spacing + width]
                window = window.reshape(-1, windows.shape[-1])
                terms.append(
                    lax.dot_general(
                        window, flat_delta, (((0,), (0,)), ((), ())), preferred_element_type=jnp.float32
                    )
                )
    scale = (count * height * width * n_row * n_col) ** (-0.5)
    gate_part, dilated_part = scattered_sum(jnp.stack(terms), scale)
    return (hidden, gate_part, dilated_part)


def scattered_sum(terms, scale):
    yh, x, c, yl, z = (lax.axis_size(a) for a in ROWS + COLS)
    lanes = terms.shape[-1]
    span = terms.size // 2 // lanes // (yh * x * c * yl)
    terms = terms.reshape(2, yh, x, c, yl, span, lanes)
    core = lax.axis_index("c")
    mine = lax.dynamic_index_in_dim(terms, core, 3, keepdims=False)
    theirs = lax.dynamic_index_in_dim(terms, 1 - core, 3, keepdims=False)
    both = mine + lax.ppermute(theirs, "c", [(0, 1), (1, 0)])
    sends = jnp.transpose(both.astype(jnp.bfloat16), (2, 3, 0, 1, 4, 5)).reshape(x * yl, -1, lanes)
    arrived = lax.all_to_all(sends, ("x", "yl"), 0, 0)
    part = jnp.sum(arrived.astype(jnp.float32), axis=0).reshape(2, yh, span, lanes)
    share = span * lanes // z
    tall = -(-(share + lanes // 2) // lanes)
    starts = [i * share // lanes for i in range(z)]
    sends = jnp.stack([part[:, :, s : s + tall] for s in starts])
    sends = jnp.transpose(sends, (2, 0, 1, 3, 4)).reshape(yh * z, 2 * tall, lanes)
    sends = jnp.pad(sends, ((0, 0), (0, -2 * tall % 8), (0, 0)))
    arrived = lax.all_to_all(sends, ("yh", "z"), 0, 0)
    total = jnp.sum(arrived[:, : 2 * tall], axis=0).reshape(2, tall * lanes) * scale
    skip = lax.axis_index("z") * share % lanes
    total = lax.dynamic_slice_in_dim(total, skip, share, axis=1)
    return total[0], total[1]


def solution(mesh):
    fine = Mesh(mesh.devices.reshape(2, 4, 2, 4, 8), ROWS + COLS)
    cells = P(None, ROWS, COLS, None)
    return jax.shard_map(
        on_device,
        mesh=fine,
        in_specs=(cells, P(), P(), cells, P(), P(), P()),
        out_specs=(cells, P(ROWS + COLS), P(ROWS + COLS)),
        check_vma=False,
    )
```

```python
import jax
import jax.numpy as jnp
from jax import lax
from jax.experimental import pallas as pl
from jax.experimental.pallas import tpu as pltpu
from jax.sharding import Mesh
from jax.sharding import PartitionSpec as P

ROWS = ("yh", "x", "c")
COLS = ("yl", "z")


def turned(cells):
    return jnp.transpose(cells, (0, 2, 1, 3))


def halos(state, seam_face, seam_code, corner_mask):
    count, height, width, _ = state.shape
    n_row = lax.axis_size(ROWS)
    n_col = lax.axis_size(COLS)
    r = lax.axis_index(ROWS)
    k = lax.axis_index(COLS)
    row_last = n_row - 1
    col_last = n_col - 1
    everywhere = ROWS + COLS
    top, bottom = r == 0, r == row_last
    west_end, east_end = k == 0, k == col_last

    def place(i, j):
        return i * n_col + j

    north, south = state[:, :2], state[:, height - 2 :]
    west, east = state[:, :, :2], state[:, :, width - 2 :]
    own_row = turned(jnp.where(top, north, jnp.flip(south, 1)))
    own_col = jnp.where(west_end, west, jnp.flip(east, 2))
    own = jnp.concatenate([own_row, own_col], axis=1)
    edges = [
        (i, j) for i in range(n_row) for j in range(n_col) if i in (0, row_last) or j in (0, col_last)
    ]

    def image(flip_row, flip_col):
        pairs = [
            (place(i, j), place(row_last - i if flip_row else i, col_last - j if flip_col else j))
            for i, j in edges
        ]
        got = lax.ppermute(own, everywhere, pairs)
        return got[:, :width], got[:, width:]

    from_above = lax.ppermute(south, ROWS, [(i, i + 1) for i in range(row_last)])
    from_below = lax.ppermute(north, ROWS, [(i + 1, i) for i in range(row_last)])
    row_x, col_x = image(False, True)
    row_y, col_y = image(True, False)
    row_xy, col_xy = image(True, True)

    def picked(options, index):
        options = jnp.stack(options)
        return jnp.take(options.reshape((4 * count,) + options.shape[2:]), index, axis=0)

    flip_x, flip_xy = jnp.flip(row_x, 1), jnp.flip(row_xy, 1)
    row_index = jnp.where(
        top, seam_code[:, 0] * count + seam_face[:, 0], seam_code[:, 1] * count + seam_face[:, 1]
    )
    row_pick = picked(
        [
            jnp.where(top, own_row, row_y),
            jnp.where(top, flip_x, flip_xy),
            jnp.where(top, row_y, own_row),
            jnp.where(top, flip_xy, flip_x),
        ],
        row_index,
    )
    row_pick = turned(row_pick)
    above = jnp.where(top, jnp.flip(row_pick, 1), from_above)
    below = jnp.where(bottom, row_pick, from_below)

    col_index = jnp.where(
        west_end, seam_code[:, 2] * count + seam_face[:, 2], seam_code[:, 3] * count + seam_face[:, 3]
    )
    flip_y, flip_xy = jnp.flip(col_y, 1), jnp.flip(col_xy, 1)
    col_pick = picked(
        [
            jnp.where(west_end, own_col, col_x),
            jnp.where(west_end, flip_y, flip_xy),
            jnp.where(west_end, col_x, own_col),
            jnp.where(west_end, flip_xy, flip_y),
        ],
        col_index,
    )

    to_right = jnp.concatenate([above[:, :, width - 2 :], east, below[:, :, width - 2 :]], axis=1)
    to_left = jnp.concatenate([above[:, :, :2], west, below[:, :, :2]], axis=1)
    from_left = lax.ppermute(to_right, COLS, [(j, j + 1) for j in range(col_last)])
    from_right = lax.ppermute(to_left, COLS, [(j + 1, j) for j in range(col_last)])
    half = n_row // 2
    along = [(i, j) for i in range(row_last) if i != half - 1 for j in (0, col_last)]
    end_above = lax.ppermute(
        col_pick[:, height - 2 :], everywhere, [(place(i, j), place(i + 1, j)) for i, j in along]
    )
    end_below = lax.ppermute(
        col_pick[:, :2], everywhere, [(place(i + 1, j), place(i, j)) for i, j in along]
    )

    def rows_of(cols):
        return jnp.where(r == half, cols[:, height - 2 :], cols[:, :2])

    back, back_x = jnp.flip(own_col, 1), jnp.flip(col_x, 1)
    middle = [
        jnp.where(west_end, rows_of(col_y), rows_of(col_xy)),
        jnp.where(west_end, rows_of(back), rows_of(back_x)),
        jnp.where(west_end, rows_of(col_xy), rows_of(col_y)),
        jnp.where(west_end, rows_of(back_x), rows_of(back)),
    ]

    def block(rows, is_west):
        cells = jnp.where(is_west, rows[:, :2], jnp.flip(rows[:, width - 2 :], 1))
        return turned(cells)

    corner = [
        block(own_row, west_end),
        block(row_x, ~west_end),
        block(row_y, west_end),
        block(row_xy, ~west_end),
    ]
    down = bottom.astype(jnp.int32)
    right = east_end.astype(jnp.int32)
    code = jnp.where(west_end, seam_code[:, 2], seam_code[:, 3])
    face = jnp.where(west_end, seam_face[:, 2], seam_face[:, 3])
    side = down ^ (code & 1)
    inner_code = jnp.where(side == 0, seam_code[face, 0], seam_code[face, 1])
    inner_face = jnp.where(side == 0, seam_face[face, 0], seam_face[face, 1])
    column = (code >> 1) ^ (inner_code & 1)
    which = 2 * ((inner_code >> 1) ^ down) + (column ^ right)
    corner_index = which * count + inner_face

    in_corner = top | bottom
    ends = picked(
        [jnp.where(in_corner, a, b) for a, b in zip(corner, middle)],
        jnp.where(in_corner, corner_index, col_index),
    )
    mask = jnp.where(
        top,
        jnp.where(west_end, corner_mask[:, 0], corner_mask[:, 1]),
        jnp.where(west_end, corner_mask[:, 2], corner_mask[:, 3]),
    )
    ends = jnp.where((in_corner & (mask == 0))[:, None, None, None], 0, ends)
    end_above = jnp.where(top, jnp.flip(ends, 1), jnp.where(r == half, ends, end_above))
    end_below = jnp.where(bottom | (r == half - 1), ends, end_below)
    edge = jnp.concatenate([end_above, col_pick, end_below], axis=1)
    left = turned(jnp.where(west_end, jnp.flip(edge, 2), from_left))
    right = turned(jnp.where(east_end, edge, from_right))

    upper = jnp.concatenate([left[:, :, :2], turned(above), right[:, :, :2]], axis=1)
    lower = jnp.concatenate([left[:, :, height + 2 :], turned(below), right[:, :, height + 2 :]], axis=1)
    return left[:, :, 2 : height + 2], right[:, :, 2 : height + 2], upper, lower


def compute_kernel(st_ref, lf_ref, rt_ref, up_ref, lo_ref, wg_ref, wd_ref, hg_ref, hidden_ref, out_ref, x_ref, dg_ref, dv_ref):
    _, faces, wide, height, c_in = x_ref.shape
    width = wide - 4
    c_out = hg_ref.shape[-1]
    dg_ref[...] = jnp.zeros(dg_ref.shape, dg_ref.dtype)
    dv_ref[...] = jnp.zeros(dv_ref.shape, dv_ref.dtype)
    step = 1
    cells = step * width * height

    def forward(n, _):
        f = n * step
        here = pl.ds(f, step)

        mid = jnp.concatenate([lf_ref[here], st_ref[here], rt_ref[here]], axis=1)
        x_ref[2, here] = mid
        mid = mid.astype(jnp.float32)
        above = up_ref[here].astype(jnp.float32)
        below = lo_ref[here].astype(jnp.float32)
        for shift, parts in (
            (0, [above, mid[:, :, : height - 2]]),
            (1, [above[:, :, 1:], mid[:, :, : height - 1]]),
            (3, [mid[:, :, 1:], below[:, :, :1]]),
            (4, [mid[:, :, 2:], below]),
        ):
            x_ref[shift, here] = jnp.concatenate(parts, axis=2).astype(jnp.bfloat16)

        def windows(spacing, first):
            return jnp.concatenate(
                [
                    x_ref[first + a * spacing, here, pl.ds(first + b * spacing, width)].reshape(cells, c_in)
                    for a in range(3)
                    for b in range(3)
                ],
                axis=1,
            )

        gate = jnp.dot(windows(1, 1), wg_ref[...], preferred_element_type=jnp.float32)
        value = jnp.dot(windows(2, 0), wd_ref[...], preferred_element_type=jnp.float32)
        root = (2.0 / jnp.pi) ** 0.5
        square = gate * gate
        t = jnp.tanh(root * gate * (1.0 + 0.044715 * square))
        half = 0.5 * (1.0 + t)
        act = gate * half
        slope = half + 0.5 * gate * (1.0 - t * t) * (root * (1.0 + 3 * 0.044715 * square))
        shape = (step, width, height, c_out)
        up = hg_ref[here].astype(jnp.float32).reshape(cells, c_out)
        hidden_ref[here] = (act * value).astype(jnp.bfloat16).reshape(shape)
        dgate = (up * value * slope).astype(jnp.bfloat16).reshape(shape)
        dvalue = (up * act).astype(jnp.bfloat16).reshape(shape)
        for b in range(3):
            lanes = pl.ds(b * c_out, c_out)
            dg_ref[here, pl.ds(b, width), :, lanes] = dgate
            dv_ref[here, pl.ds(2 * b, width), :, lanes] = dvalue
        return 0

    lax.fori_loop(0, faces // step, forward, 0, unroll=True)

    span = out_ref.shape[3]

    def put(grad, tap, block):
        start, end = tap * c_in, (tap + 1) * c_in
        at = start
        while at < end:
            chunk = at // span
            stop = min(end, (chunk + 1) * span)
            out_ref[chunk % 2, chunk // 2, grad, pl.ds(at - chunk * span, stop - at)] = block[at - start : stop - start]
            at = stop

    for a in range(3):
        for grad, row, cols, delta in ((0, 1 + a, pl.ds(1, wide - 2), dg_ref), (1, 2 * a, pl.ds(0, wide), dv_ref)):
            x = x_ref[row, :, cols].reshape(-1, c_in)
            d = delta[...].reshape(-1, 3 * c_out)
            sums = lax.dot_general(x, d, (((0,), (0,)), ((), ())), preferred_element_type=jnp.float32)
            for b in range(3):
                put(grad, a * 3 + b, sums[:, b * c_out : (b + 1) * c_out])


def compute(st, lf, rt, up, lo, wg, wd, hg):
    faces, width, height, c_in = st.shape
    wide = width + 4
    c_out = wg.shape[-1]
    vm = pl.BlockSpec(memory_space=pltpu.VMEM)
    return pl.pallas_call(
        compute_kernel,
        in_specs=[vm] * 8,
        out_specs=[vm] * 2,
        out_shape=[
            jax.ShapeDtypeStruct(hg.shape, jnp.bfloat16),
            jax.ShapeDtypeStruct((2, 8, 2, 9 * c_in // 16, c_out), jnp.float32),
        ],
        scratch_shapes=[
            pltpu.VMEM((5, faces, wide, height, c_in), jnp.bfloat16),
            pltpu.VMEM((faces, wide - 2, height, 3 * c_out), jnp.bfloat16),
            pltpu.VMEM((faces, wide, height, 3 * c_out), jnp.bfloat16),
        ],
        compiler_params=pltpu.CompilerParams(vmem_limit_bytes=56 * 2**20),
        name="gated_conv",
    )(st, lf, rt, up, lo, wg.reshape(-1, c_out), wd.reshape(-1, c_out), hg)


def on_device(state, gate_kernel, dilated_kernel, hidden_grad, seam_face, seam_code, corner_mask):
    count, height, width, _ = state.shape
    left, right, upper, lower = halos(state, seam_face, seam_code, corner_mask)
    hidden, terms = compute(
        turned(state), left, right, upper, lower, gate_kernel, dilated_kernel, turned(hidden_grad)
    )
    cells = count * height * width * lax.axis_size(ROWS) * lax.axis_size(COLS)
    gate_part, dilated_part = scattered_sum(terms, cells ** (-0.5))
    return (turned(hidden), gate_part, dilated_part)


def scattered_sum(terms, scale):
    _, spots, grads, span, lanes = terms.shape
    halves = lax.all_to_all(terms, "c", 0, 0)
    sends = (halves[0] + halves[1]).astype(jnp.bfloat16).reshape(spots, grads * span, lanes)
    arrived = lax.all_to_all(sends, ("yh", "x"), 0, 0)
    part = jnp.sum(arrived.astype(jnp.float32), axis=0).reshape(grads, span, lanes)
    takers = lax.axis_size(COLS)
    share = span * lanes // takers
    tall = -(-(share + lanes // 2) // lanes)
    starts = [i * share // lanes for i in range(takers)]
    sends = jnp.stack([part[:, s : s + tall].reshape(grads * tall, lanes) for s in starts])
    sends = jnp.pad(sends, ((0, 0), (0, -grads * tall % 8), (0, 0)))
    arrived = lax.all_to_all(sends, COLS, 0, 0)
    total = jnp.sum(arrived[:, : grads * tall], axis=0).reshape(grads, tall * lanes) * scale
    skip = lax.axis_index(COLS) * share % lanes
    total = lax.dynamic_slice_in_dim(total, skip, share, axis=1)
    return total[0], total[1]


def solution(mesh):
    fine = Mesh(mesh.devices.reshape(2, 4, 2, 4, 8), ROWS + COLS)
    cells = P(None, ROWS, COLS, None)
    return jax.shard_map(
        on_device,
        mesh=fine,
        in_specs=(cells, P(), P(), cells, P(), P(), P()),
        out_specs=(cells, P(ROWS + COLS), P(ROWS + COLS)),
        check_vma=False,
    )
```

```python
import jax
import jax.numpy as jnp
from jax import lax
from jax.experimental import pallas as pl
from jax.experimental.pallas import tpu as pltpu
from jax.sharding import Mesh
from jax.sharding import PartitionSpec as P

ROWS = ("yh", "x", "c")
COLS = ("yl", "z")


def turned(cells):
    return jnp.transpose(cells, (0, 2, 1, 3))


def chosen(table, index):
    return table.at[index].get(mode="promise_in_bounds")


def looked_up(table, index):
    spots = jnp.arange(table.shape[0])
    return jnp.sum(jnp.where(index[:, None] == spots[None, :], table[None, :], 0), axis=1)


def per_face(condition, yes, no):
    return jnp.where(condition[:, None, None, None], yes, no)


def halos(cells, seam_face, seam_code, corner_mask):
    count, width, height, _ = cells.shape
    n_row = lax.axis_size(ROWS)
    n_col = lax.axis_size(COLS)
    r = lax.axis_index(ROWS)
    k = lax.axis_index(COLS)
    row_last = n_row - 1
    col_last = n_col - 1
    everywhere = ROWS + COLS
    top, bottom = r == 0, r == row_last
    west_end, east_end = k == 0, k == col_last
    down = bottom.astype(jnp.int32)
    right = east_end.astype(jnp.int32)
    in_corner = (top | bottom) & (west_end | east_end)
    corners = [(i, j) for i in (0, row_last) for j in (0, col_last)]
    edge_rows = [(i, j) for i in (0, row_last) for j in range(1, col_last)]
    edge_cols = [(i, j) for i in range(1, row_last) for j in (0, col_last)]

    def swap(x, where, image):
        pairs = []
        for i, j in where:
            other = (row_last - i if image & 2 else i) * n_col + (col_last - j if image & 1 else j)
            pairs.append((i * n_col + j, other))
        return lax.ppermute(x, everywhere, pairs)

    north, south = cells[:, :, :2], cells[:, :, height - 2 :]
    from_above = lax.ppermute(south, ROWS, [(i, i + 1) for i in range(row_last)])
    from_below = lax.ppermute(north, ROWS, [(i + 1, i) for i in range(row_last)])

    own_row = jnp.where(top, north, jnp.flip(south, 2))

    def side_columns(above, below, columns):
        return jnp.concatenate([above[:, columns], cells[:, columns], below[:, columns]], axis=2)

    west, east = slice(0, 2), slice(width - 2, width)
    own_col = jnp.where(
        west_end,
        side_columns(from_above, from_below, west),
        jnp.flip(side_columns(from_above, from_below, east), 1),
    )
    tall = height + 4
    row_image = swap(own_row, edge_rows, 1)
    col_image = swap(own_col, edge_cols, 3)
    both_image = swap(jnp.concatenate([own_col, turned(own_row)], axis=2), corners, 3)
    row_image = jnp.where(in_corner, turned(both_image[:, :, tall:]), row_image)
    col_image = jnp.where(in_corner, both_image[:, :, :tall], col_image)

    def row_seam(is_top):
        code = jnp.where(is_top, seam_code[:, 0], seam_code[:, 1])
        face = jnp.where(is_top, seam_face[:, 0], seam_face[:, 1])
        side = jnp.where(is_top, 0, 1)
        return 2 * ((code >> 1) ^ side) + (code & 1), face

    row_first = jnp.where(in_corner, 3, 1)
    row_next = jnp.where(in_corner, 1, 2)
    row_from, row_face = row_seam(top)
    give_from, give_face = row_seam(jnp.where(in_corner, top, ~top))

    def column_seam(is_west):
        code = jnp.where(is_west, seam_code[:, 2], seam_code[:, 3])
        face = jnp.where(is_west, seam_face[:, 2], seam_face[:, 3])
        at = jnp.where(is_west, 0, 1)
        side = down ^ (code & 1)
        inner = jnp.where(side == 0, looked_up(seam_code[:, 0], face), looked_up(seam_code[:, 1], face))
        inner_face = jnp.where(side == 0, looked_up(seam_face[:, 0], face), looked_up(seam_face[:, 1], face))
        inner_east = (code >> 1) ^ (inner & 1)
        inner_from = 2 * ((inner >> 1) ^ down) + (inner_east ^ at)
        return 2 * (code & 1) + ((code >> 1) ^ at), face, inner_from, inner_face, inner_east

    col_from, col_face, block_from, block_face, block_east = column_seam(west_end)
    give_col, give_col_face, give_block, give_block_face, give_east = column_seam(~west_end)

    def spot(comes_from, first, face):
        return jnp.where(comes_from == first, count, 0) + face

    row_all = chosen(
        jnp.concatenate([own_row, row_image]),
        jnp.concatenate(
            [
                spot(row_from, row_first, row_face),
                spot(give_from ^ row_next, row_first, give_face),
                spot(block_from, 3, block_face),
                spot(give_block ^ 1, 3, give_block_face),
            ]
        ),
    )
    col_all = chosen(
        jnp.concatenate([own_col, col_image]),
        jnp.concatenate([spot(col_from, 3, col_face), spot(give_col ^ 1, 3, give_col_face)]),
    )

    def block(rows, is_east):
        return per_face(is_east == 0, rows[:, west], jnp.flip(rows[:, east], 1))

    row_here, row_gift = row_all[:count], row_all[count : 2 * count]
    block_here = block(row_all[2 * count : 3 * count], block_east)
    col_here = col_all[:count]
    col_gift, block_gift = col_all[count:], block(row_all[3 * count :], give_east)
    row_given = swap(row_gift, edge_rows, 2)
    col_given = swap(col_gift, edge_cols, 1)
    both_given = swap(jnp.concatenate([col_gift, turned(row_gift), block_gift], axis=2), corners, 1)
    row_given = jnp.where(in_corner, turned(both_given[:, :, tall : tall + width]), row_given)
    col_given = jnp.where(in_corner, both_given[:, :, :tall], col_given)
    block_given = both_given[:, :, tall + width :]

    def at_hand(comes_from, first):
        return (comes_from == 0) | (comes_from == first)

    row_pick = per_face(at_hand(row_from, row_first), row_here, row_given)
    row_pick = per_face(row_from & 1 == 1, jnp.flip(row_pick, 1), row_pick)
    above = jnp.where(top, jnp.flip(row_pick, 2), from_above)
    below = jnp.where(bottom, row_pick, from_below)
    from_left = lax.ppermute(side_columns(above, below, east), COLS, [(j, j + 1) for j in range(col_last)])
    from_right = lax.ppermute(side_columns(above, below, west), COLS, [(j + 1, j) for j in range(col_last)])

    col_pick = per_face(at_hand(col_from, 3), col_here, col_given)
    col_pick = per_face(col_from & 2 == 2, jnp.flip(col_pick, 2), col_pick)
    corner = per_face(at_hand(block_from, 3), block_here, block_given)
    mask = jnp.where(
        top,
        jnp.where(west_end, corner_mask[:, 0], corner_mask[:, 1]),
        jnp.where(west_end, corner_mask[:, 2], corner_mask[:, 3]),
    )
    corner = per_face(mask == 0, 0, corner)
    edge = jnp.concatenate(
        [
            jnp.where(top, jnp.flip(corner, 2), col_pick[:, :, :2]),
            col_pick[:, :, 2 : height + 2],
            jnp.where(bottom, corner, col_pick[:, :, height + 2 :]),
        ],
        axis=2,
    )
    left_cols = jnp.where(west_end, jnp.flip(edge, 1), from_left)
    right_cols = jnp.where(east_end, edge, from_right)
    return left_cols, right_cols, above, below


def compute_kernel(
    core_ref,
    st_ref,
    lf_ref,
    rt_ref,
    up_ref,
    lo_ref,
    wg_ref,
    wd_ref,
    hg_ref,
    hidden_ref,
    mine_ref,
    theirs_ref,
    x_ref,
    dg_ref,
    dv_ref,
    sums_ref,
    sems,
):
    _, faces, wide, height, c_in = x_ref.shape
    width = wide - 4
    c_out = hg_ref.shape[-1]
    dg_ref[...] = jnp.zeros(dg_ref.shape, dg_ref.dtype)
    dv_ref[...] = jnp.zeros(dv_ref.shape, dv_ref.dtype)
    step = 1
    cells = step * width * height

    def forward(n, _):
        f = n * step
        here = pl.ds(f, step)

        inside = pl.ds(2, width)
        mid = st_ref[here]
        x_ref[2, here, inside] = mid
        mid = mid.astype(jnp.float32)
        above = up_ref[here].astype(jnp.float32)
        below = lo_ref[here].astype(jnp.float32)
        left = lf_ref[here].astype(jnp.float32)
        right = rt_ref[here].astype(jnp.float32)
        for shift in range(5):
            rows = slice(shift, shift + height)
            x_ref[shift, here, pl.ds(0, 2)] = left[:, :, rows].astype(jnp.bfloat16)
            x_ref[shift, here, pl.ds(width + 2, 2)] = right[:, :, rows].astype(jnp.bfloat16)
        for shift, parts in (
            (0, [above, mid[:, :, : height - 2]]),
            (1, [above[:, :, 1:], mid[:, :, : height - 1]]),
            (3, [mid[:, :, 1:], below[:, :, :1]]),
            (4, [mid[:, :, 2:], below]),
        ):
            x_ref[shift, here, inside] = jnp.concatenate(parts, axis=2).astype(jnp.bfloat16)

        def windows(spacing, first):
            return jnp.concatenate(
                [
                    x_ref[first + a * spacing, here, pl.ds(first + b * spacing, width)].reshape(cells, c_in)
                    for a in range(3)
                    for b in range(3)
                ],
                axis=1,
            )

        gate = jnp.dot(windows(1, 1), wg_ref[...], preferred_element_type=jnp.float32)
        value = jnp.dot(windows(2, 0), wd_ref[...], preferred_element_type=jnp.float32)
        root = (2.0 / jnp.pi) ** 0.5
        square = gate * gate
        t = jnp.tanh(root * gate * (1.0 + 0.044715 * square))
        half = 0.5 * (1.0 + t)
        act = gate * half
        slope = half + 0.5 * gate * (1.0 - t * t) * (root * (1.0 + 3 * 0.044715 * square))
        shape = (step, width, height, c_out)
        up = hg_ref[here].astype(jnp.float32).reshape(cells, c_out)
        hidden_ref[here] = (act * value).astype(jnp.bfloat16).reshape(shape)
        dgate = (up * value * slope).astype(jnp.bfloat16).reshape(shape)
        dvalue = (up * act).astype(jnp.bfloat16).reshape(shape)
        for b in range(3):
            lanes = pl.ds(b * c_out, c_out)
            dg_ref[here, pl.ds(b, width), :, lanes] = dgate
            dv_ref[here, pl.ds(2 * b, width), :, lanes] = dvalue
        return 0

    lax.fori_loop(0, faces // step, forward, 0, unroll=True)

    grads, _, across, along, span, _ = sums_ref.shape

    def put(grad, tap, block):
        start, end = tap * c_in, (tap + 1) * c_in
        at = start
        while at < end:
            n = at // span
            stop = min(end, (n + 1) * span)
            spot = n // 2 % across, n // 2 // across
            sums_ref[grad, n % 2, spot[0], spot[1], pl.ds(at - n * span, stop - at)] = block[at - start : stop - start]
            at = stop

    core = core_ref[0]
    copies = []
    for grad, first, cols, delta in ((0, 1, pl.ds(1, wide - 2), dg_ref), (1, 0, pl.ds(0, wide), dv_ref)):
        d = delta[...].reshape(-1, 3 * c_out)
        for a in range(3):
            x = x_ref[first + a * (grad + 1), :, cols].reshape(-1, c_in)
            sums = lax.dot_general(x, d, (((0,), (0,)), ((), ())), preferred_element_type=jnp.float32)
            for b in range(3):
                put(grad, a * 3 + b, sums[:, b * c_out : (b + 1) * c_out])
        for n, target in ((core, mine_ref), (1 - core, theirs_ref)):
            copy = pltpu.make_async_copy(sums_ref.at[grad, n], target.at[grad], sems.at[len(copies)])
            copy.start()
            copies.append(copy)
    for copy in copies:
        copy.wait()


def compute(core, st, lf, rt, up, lo, wg, wd, hg):
    faces, width, height, c_in = st.shape
    wide = width + 4
    c_out = wg.shape[-1]
    across, along = lax.axis_size("x"), lax.axis_size("yh")
    shares = (2, across, along, 9 * c_in // (2 * across * along), c_out)
    vm = pl.BlockSpec(memory_space=pltpu.VMEM)
    anywhere = pl.BlockSpec(memory_space=pl.ANY)
    return pl.pallas_call(
        compute_kernel,
        in_specs=[pl.BlockSpec(memory_space=pltpu.SMEM)] + [vm] * 8,
        out_specs=[vm, anywhere, anywhere],
        out_shape=[
            jax.ShapeDtypeStruct(hg.shape, jnp.bfloat16),
            jax.ShapeDtypeStruct(shares, jnp.float32),
            jax.ShapeDtypeStruct(shares, jnp.float32),
        ],
        scratch_shapes=[
            pltpu.VMEM((5, faces, wide, height, c_in), jnp.bfloat16),
            pltpu.VMEM((faces, wide - 2, height, 3 * c_out), jnp.bfloat16),
            pltpu.VMEM((faces, wide, height, 3 * c_out), jnp.bfloat16),
            pltpu.VMEM((2,) + shares, jnp.float32),
            pltpu.SemaphoreType.DMA((4,)),
        ],
        compiler_params=pltpu.CompilerParams(vmem_limit_bytes=56 * 2**20),
        name="gated_conv",
    )(core, st, lf, rt, up, lo, wg.reshape(-1, c_out), wd.reshape(-1, c_out), hg)


def on_device(state, gate_kernel, dilated_kernel, hidden_grad, seam_face, seam_code, corner_mask):
    count, height, width, _ = state.shape
    cells = turned(state)
    left, right, above, below = halos(cells, seam_face, seam_code, corner_mask)
    core = lax.axis_index("c").reshape(1)
    hidden, mine, theirs = compute(
        core, cells, left, right, above, below, gate_kernel, dilated_kernel, turned(hidden_grad)
    )
    total_cells = count * height * width * lax.axis_size(ROWS) * lax.axis_size(COLS)
    gate_part, dilated_part = scattered_sum(mine, theirs, total_cells ** (-0.5))
    return (turned(hidden), gate_part, dilated_part)


def scattered_sum(mine, theirs, scale):
    both = mine + lax.ppermute(theirs, "c", [(0, 1), (1, 0)])
    grads, across, along, span, lanes = both.shape
    sends = jnp.transpose(both.astype(jnp.bfloat16), (1, 0, 2, 3, 4))
    arrived = lax.all_to_all(sends.reshape(across, -1, lanes), "x", 0, 0)
    part = jnp.sum(arrived.astype(jnp.float32), axis=0).reshape(grads, along, span, lanes)
    takers = lax.axis_size(COLS)
    share = span * lanes // takers
    tall = -(-(share + lanes // 2) // lanes)
    starts = [i * share // lanes for i in range(takers)]
    sends = jnp.stack([part[:, :, s : s + tall] for s in starts])
    sends = jnp.transpose(sends, (2, 0, 3, 1, 4)).reshape(along * takers, tall, grads, lanes)
    arrived = lax.all_to_all(sends, ("yh",) + COLS, 0, 0)
    total = jnp.transpose(jnp.sum(arrived, axis=0) * scale, (1, 0, 2)).reshape(grads, tall * lanes)
    skip = lax.axis_index(COLS) * share % lanes
    total = lax.dynamic_slice_in_dim(total, skip, share, axis=1)
    return total[0], total[1]


def solution(mesh):
    fine = Mesh(mesh.devices.reshape(2, 4, 2, 4, 8), ROWS + COLS)
    cells = P(None, ROWS, COLS, None)
    return jax.shard_map(
        on_device,
        mesh=fine,
        in_specs=(cells, P(), P(), cells, P(), P(), P()),
        out_specs=(cells, P(ROWS + COLS), P(ROWS + COLS)),
        check_vma=False,
    )
```

```python
import jax
import jax.numpy as jnp
from jax import lax
from jax.experimental import pallas as pl
from jax.experimental.pallas import tpu as pltpu
from jax.sharding import Mesh
from jax.sharding import PartitionSpec as P

ROWS = ("yh", "x", "c")
COLS = ("yl", "z")


def turned(cells):
    return jnp.transpose(cells, (0, 2, 1, 3))


def chosen(table, index):
    return table.at[index].get(mode="promise_in_bounds")


def looked_up(table, index):
    spots = jnp.arange(table.shape[0])
    return jnp.sum(jnp.where(index[:, None] == spots[None, :], table[None, :], 0), axis=1)


def per_face(condition, yes, no):
    return jnp.where(condition[:, None, None, None], yes, no)


def halos(cells, seam_face, seam_code, corner_mask):
    count, width, height, _ = cells.shape
    n_row = lax.axis_size(ROWS)
    n_col = lax.axis_size(COLS)
    r = lax.axis_index(ROWS)
    k = lax.axis_index(COLS)
    row_last = n_row - 1
    col_last = n_col - 1
    everywhere = ROWS + COLS
    top, bottom = r == 0, r == row_last
    west_end, east_end = k == 0, k == col_last
    down = bottom.astype(jnp.int32)
    right = east_end.astype(jnp.int32)
    in_corner = (top | bottom) & (west_end | east_end)
    corners = [(i, j) for i in (0, row_last) for j in (0, col_last)]
    edge_rows = [(i, j) for i in (0, row_last) for j in range(1, col_last)]
    edge_cols = [(i, j) for i in range(1, row_last) for j in (0, col_last)]

    def late(i):
        return i % 2 ^ i // (n_row // 2)

    def swap(x, where, image, late_image=None):
        pairs = []
        for i, j in where:
            to = late_image if late_image and late(i) else image
            other = (row_last - i if to & 2 else i) * n_col + (col_last - j if to & 1 else j)
            pairs.append((i * n_col + j, other))
        return lax.ppermute(x, everywhere, pairs)

    north, south = cells[:, :, :2], cells[:, :, height - 2 :]
    from_above = lax.ppermute(south, ROWS, [(i, i + 1) for i in range(row_last)])
    from_below = lax.ppermute(north, ROWS, [(i + 1, i) for i in range(row_last)])

    def side_columns(above, below, columns):
        return jnp.concatenate([above[:, columns], cells[:, columns], below[:, columns]], axis=2)

    west, east = slice(0, 2), slice(width - 2, width)

    def sideways(above, below, rows):
        steps = [(i * n_col + j, i * n_col + j + 1) for i in rows for j in range(col_last)]
        from_left = lax.ppermute(side_columns(above, below, east), everywhere, steps)
        from_right = lax.ppermute(side_columns(above, below, west), everywhere, [(b, a) for a, b in steps])
        return from_left, from_right

    left_inner, right_inner = sideways(from_above, from_below, range(1, row_last))

    own_row = jnp.where(top, north, jnp.flip(south, 2))

    own_col = jnp.where(
        west_end,
        side_columns(from_above, from_below, west),
        jnp.flip(side_columns(from_above, from_below, east), 1),
    )
    tall = height + 4
    row_image = swap(own_row, edge_rows, 1)
    col_image = swap(own_col, edge_cols, 3, 1)
    both_image = swap(jnp.concatenate([own_col, turned(own_row)], axis=2), corners, 3)
    row_image = jnp.where(in_corner, turned(both_image[:, :, tall:]), row_image)
    col_image = jnp.where(in_corner, both_image[:, :, :tall], col_image)

    def row_seam(is_top):
        code = jnp.where(is_top, seam_code[:, 0], seam_code[:, 1])
        face = jnp.where(is_top, seam_face[:, 0], seam_face[:, 1])
        side = jnp.where(is_top, 0, 1)
        return 2 * ((code >> 1) ^ side) + (code & 1), face

    col_late = ~in_corner & (late(r) == 1)
    col_first = jnp.where(col_late, 1, 3)
    col_next = jnp.where(col_late, 3, 1)
    row_first = jnp.where(in_corner, 3, 1)
    row_next = jnp.where(in_corner, 1, 2)
    row_from, row_face = row_seam(top)
    give_from, give_face = row_seam(jnp.where(in_corner, top, ~top))

    def column_seam(is_west):
        code = jnp.where(is_west, seam_code[:, 2], seam_code[:, 3])
        face = jnp.where(is_west, seam_face[:, 2], seam_face[:, 3])
        at = jnp.where(is_west, 0, 1)
        side = down ^ (code & 1)
        inner = jnp.where(side == 0, looked_up(seam_code[:, 0], face), looked_up(seam_code[:, 1], face))
        inner_face = jnp.where(side == 0, looked_up(seam_face[:, 0], face), looked_up(seam_face[:, 1], face))
        inner_east = (code >> 1) ^ (inner & 1)
        inner_from = 2 * ((inner >> 1) ^ down) + (inner_east ^ at)
        return 2 * (code & 1) + ((code >> 1) ^ at), face, inner_from, inner_face, inner_east

    col_from, col_face, block_from, block_face, block_east = column_seam(west_end)
    give_col, give_col_face, give_block, give_block_face, give_east = column_seam(~west_end)

    def spot(comes_from, first, face):
        return jnp.where(comes_from == first, count, 0) + face

    row_all = chosen(
        jnp.concatenate([own_row, row_image]),
        jnp.concatenate(
            [
                spot(row_from, row_first, row_face),
                spot(give_from ^ row_next, row_first, give_face),
                spot(block_from, 3, block_face),
                spot(give_block ^ 1, 3, give_block_face),
            ]
        ),
    )
    col_all = chosen(
        jnp.concatenate([own_col, col_image]),
        jnp.concatenate([spot(col_from, col_first, col_face), spot(give_col ^ col_next, col_first, give_col_face)]),
    )

    def block(rows, is_east):
        return per_face(is_east == 0, rows[:, west], jnp.flip(rows[:, east], 1))

    row_here, row_gift = row_all[:count], row_all[count : 2 * count]
    block_here = block(row_all[2 * count : 3 * count], block_east)
    col_here = col_all[:count]
    col_gift, block_gift = col_all[count:], block(row_all[3 * count :], give_east)
    row_given = swap(row_gift, edge_rows, 2)
    col_given = swap(col_gift, edge_cols, 1, 3)
    both_given = swap(jnp.concatenate([col_gift, turned(row_gift), block_gift], axis=2), corners, 1)
    row_given = jnp.where(in_corner, turned(both_given[:, :, tall : tall + width]), row_given)
    col_given = jnp.where(in_corner, both_given[:, :, :tall], col_given)
    block_given = both_given[:, :, tall + width :]

    def at_hand(comes_from, first):
        return (comes_from == 0) | (comes_from == first)

    row_pick = per_face(at_hand(row_from, row_first), row_here, row_given)
    row_pick = per_face(row_from & 1 == 1, jnp.flip(row_pick, 1), row_pick)
    above = jnp.where(top, jnp.flip(row_pick, 2), from_above)
    below = jnp.where(bottom, row_pick, from_below)
    left_edge, right_edge = sideways(above, below, (0, row_last))
    from_left = jnp.where(top | bottom, left_edge, left_inner)
    from_right = jnp.where(top | bottom, right_edge, right_inner)

    col_pick = per_face(at_hand(col_from, col_first), col_here, col_given)
    col_pick = per_face(col_from & 2 == 2, jnp.flip(col_pick, 2), col_pick)
    corner = per_face(at_hand(block_from, 3), block_here, block_given)
    mask = jnp.where(
        top,
        jnp.where(west_end, corner_mask[:, 0], corner_mask[:, 1]),
        jnp.where(west_end, corner_mask[:, 2], corner_mask[:, 3]),
    )
    corner = per_face(mask == 0, 0, corner)
    edge = jnp.concatenate(
        [
            jnp.where(top, jnp.flip(corner, 2), col_pick[:, :, :2]),
            col_pick[:, :, 2 : height + 2],
            jnp.where(bottom, corner, col_pick[:, :, height + 2 :]),
        ],
        axis=2,
    )
    left_cols = jnp.where(west_end, jnp.flip(edge, 1), from_left)
    right_cols = jnp.where(east_end, edge, from_right)
    return left_cols, right_cols, above, below


def compute_kernel(
    core_ref,
    st_ref,
    lf_ref,
    rt_ref,
    up_ref,
    lo_ref,
    wg_ref,
    wd_ref,
    hg_ref,
    hidden_ref,
    mine_ref,
    theirs_ref,
    x_ref,
    dg_ref,
    dv_ref,
    sums_ref,
    sems,
):
    _, faces, wide, height, c_in = x_ref.shape
    width = wide - 4
    c_out = hg_ref.shape[-1]
    dg_ref[...] = jnp.zeros(dg_ref.shape, dg_ref.dtype)
    dv_ref[...] = jnp.zeros(dv_ref.shape, dv_ref.dtype)
    step = 1
    cells = step * width * height

    def forward(n, _):
        f = n * step
        here = pl.ds(f, step)

        inside = pl.ds(2, width)
        mid = st_ref[here]
        x_ref[2, here, inside] = mid
        mid = mid.astype(jnp.float32)
        above = up_ref[here].astype(jnp.float32)
        below = lo_ref[here].astype(jnp.float32)
        left = lf_ref[here].astype(jnp.float32)
        right = rt_ref[here].astype(jnp.float32)
        for shift in range(5):
            rows = slice(shift, shift + height)
            x_ref[shift, here, pl.ds(0, 2)] = left[:, :, rows].astype(jnp.bfloat16)
            x_ref[shift, here, pl.ds(width + 2, 2)] = right[:, :, rows].astype(jnp.bfloat16)
        for shift, parts in (
            (0, [above, mid[:, :, : height - 2]]),
            (1, [above[:, :, 1:], mid[:, :, : height - 1]]),
            (3, [mid[:, :, 1:], below[:, :, :1]]),
            (4, [mid[:, :, 2:], below]),
        ):
            x_ref[shift, here, inside] = jnp.concatenate(parts, axis=2).astype(jnp.bfloat16)

        def windows(spacing, first):
            return jnp.concatenate(
                [
                    x_ref[first + a * spacing, here, pl.ds(first + b * spacing, width)].reshape(cells, c_in)
                    for a in range(3)
                    for b in range(3)
                ],
                axis=1,
            )

        gate = jnp.dot(windows(1, 1), wg_ref[...], preferred_element_type=jnp.float32)
        value = jnp.dot(windows(2, 0), wd_ref[...], preferred_element_type=jnp.float32)
        root = (2.0 / jnp.pi) ** 0.5
        square = gate * gate
        t = jnp.tanh(root * gate * (1.0 + 0.044715 * square))
        half = 0.5 * (1.0 + t)
        act = gate * half
        slope = half + 0.5 * gate * (1.0 - t * t) * (root * (1.0 + 3 * 0.044715 * square))
        shape = (step, width, height, c_out)
        up = hg_ref[here].astype(jnp.float32).reshape(cells, c_out)
        hidden_ref[here] = (act * value).astype(jnp.bfloat16).reshape(shape)
        dgate = (up * value * slope).astype(jnp.bfloat16).reshape(shape)
        dvalue = (up * act).astype(jnp.bfloat16).reshape(shape)
        for b in range(3):
            lanes = pl.ds(b * c_out, c_out)
            dg_ref[here, pl.ds(b, width), :, lanes] = dgate
            dv_ref[here, pl.ds(2 * b, width), :, lanes] = dvalue
        return 0

    lax.fori_loop(0, faces // step, forward, 0, unroll=True)

    grads, _, across, along, span, _ = sums_ref.shape

    def put(grad, tap, block):
        start, end = tap * c_in, (tap + 1) * c_in
        at = start
        while at < end:
            n = at // span
            stop = min(end, (n + 1) * span)
            spot = n // 2 % across, n // 2 // across
            sums_ref[grad, n % 2, spot[0], spot[1], pl.ds(at - n * span, stop - at)] = block[at - start : stop - start]
            at = stop

    core = core_ref[0]
    copies = []
    for grad, first, cols, delta in ((0, 1, pl.ds(1, wide - 2), dg_ref), (1, 0, pl.ds(0, wide), dv_ref)):
        d = delta[...].reshape(-1, 3 * c_out)
        for a in range(3):
            x = x_ref[first + a * (grad + 1), :, cols].reshape(-1, c_in)
            sums = lax.dot_general(x, d, (((0,), (0,)), ((), ())), preferred_element_type=jnp.float32)
            for b in range(3):
                put(grad, a * 3 + b, sums[:, b * c_out : (b + 1) * c_out])
        for n, target in ((core, mine_ref), (1 - core, theirs_ref)):
            copy = pltpu.make_async_copy(sums_ref.at[grad, n], target.at[grad], sems.at[len(copies)])
            copy.start()
            copies.append(copy)
    for copy in copies:
        copy.wait()


def compute(core, st, lf, rt, up, lo, wg, wd, hg):
    faces, width, height, c_in = st.shape
    wide = width + 4
    c_out = wg.shape[-1]
    across, along = lax.axis_size("x"), lax.axis_size("yh")
    shares = (2, across, along, 9 * c_in // (2 * across * along), c_out)
    vm = pl.BlockSpec(memory_space=pltpu.VMEM)
    anywhere = pl.BlockSpec(memory_space=pl.ANY)
    return pl.pallas_call(
        compute_kernel,
        in_specs=[pl.BlockSpec(memory_space=pltpu.SMEM)] + [vm] * 8,
        out_specs=[vm, anywhere, anywhere],
        out_shape=[
            jax.ShapeDtypeStruct(hg.shape, jnp.bfloat16),
            jax.ShapeDtypeStruct(shares, jnp.float32),
            jax.ShapeDtypeStruct(shares, jnp.float32),
        ],
        scratch_shapes=[
            pltpu.VMEM((5, faces, wide, height, c_in), jnp.bfloat16),
            pltpu.VMEM((faces, wide - 2, height, 3 * c_out), jnp.bfloat16),
            pltpu.VMEM((faces, wide, height, 3 * c_out), jnp.bfloat16),
            pltpu.VMEM((2,) + shares, jnp.float32),
            pltpu.SemaphoreType.DMA((4,)),
        ],
        compiler_params=pltpu.CompilerParams(vmem_limit_bytes=56 * 2**20),
        name="gated_conv",
    )(core, st, lf, rt, up, lo, wg.reshape(-1, c_out), wd.reshape(-1, c_out), hg)


def on_device(state, gate_kernel, dilated_kernel, hidden_grad, seam_face, seam_code, corner_mask):
    count, height, width, _ = state.shape
    cells = turned(state)
    left, right, above, below = halos(cells, seam_face, seam_code, corner_mask)
    core = lax.axis_index("c").reshape(1)
    hidden, mine, theirs = compute(
        core, cells, left, right, above, below, gate_kernel, dilated_kernel, turned(hidden_grad)
    )
    total_cells = count * height * width * lax.axis_size(ROWS) * lax.axis_size(COLS)
    gate_part, dilated_part = scattered_sum(mine, theirs, total_cells ** (-0.5))
    return (turned(hidden), gate_part, dilated_part)


def scattered_sum(mine, theirs, scale):
    both = mine + lax.ppermute(theirs, "c", [(0, 1), (1, 0)])
    grads, across, along, span, lanes = both.shape
    sends = jnp.transpose(both.astype(jnp.bfloat16), (1, 0, 2, 3, 4))
    arrived = lax.all_to_all(sends.reshape(across, -1, lanes), "x", 0, 0)
    part = jnp.sum(arrived.astype(jnp.float32), axis=0).reshape(grads, along, span, lanes)
    takers = lax.axis_size(COLS)
    share = span * lanes // takers
    tall = -(-(share + lanes // 2) // lanes)
    starts = [i * share // lanes for i in range(takers)]
    part = part.astype(jnp.bfloat16)
    sends = jnp.stack([part[:, :, s : s + tall] for s in starts])
    sends = jnp.transpose(sends, (2, 0, 3, 1, 4)).reshape(along * takers, tall, grads, lanes)
    arrived = lax.all_to_all(sends, ("yh",) + COLS, 0, 0)
    total = jnp.transpose(jnp.sum(arrived.astype(jnp.float32), axis=0) * scale, (1, 0, 2)).reshape(grads, tall * lanes)
    skip = lax.axis_index(COLS) * share % lanes
    total = lax.dynamic_slice_in_dim(total, skip, share, axis=1)
    return total[0], total[1]


def solution(mesh):
    fine = Mesh(mesh.devices.reshape(2, 4, 2, 4, 8), ROWS + COLS)
    cells = P(None, ROWS, COLS, None)
    return jax.shard_map(
        on_device,
        mesh=fine,
        in_specs=(cells, P(), P(), cells, P(), P(), P()),
        out_specs=(cells, P(ROWS + COLS), P(ROWS + COLS)),
        check_vma=False,
    )
```

```python
import jax
import jax.numpy as jnp
from jax import lax
from jax.experimental import pallas as pl
from jax.experimental.pallas import tpu as pltpu
from jax.sharding import Mesh
from jax.sharding import PartitionSpec as P

ROWS = ("yh", "x", "c")
COLS = ("yl", "z")


def turned(cells):
    return jnp.transpose(cells, (0, 2, 1, 3))


def chosen(table, index):
    return table.at[index].get(mode="promise_in_bounds")


def looked_up(table, index):
    spots = jnp.arange(table.shape[0])
    return jnp.sum(jnp.where(index[:, None] == spots[None, :], table[None, :], 0), axis=1)


def per_face(condition, yes, no):
    return jnp.where(condition[:, None, None, None], yes, no)


def halos(cells, seam_face, seam_code, corner_mask):
    count, width, height, _ = cells.shape
    n_row = lax.axis_size(ROWS)
    n_col = lax.axis_size(COLS)
    r = lax.axis_index(ROWS)
    k = lax.axis_index(COLS)
    row_last = n_row - 1
    col_last = n_col - 1
    everywhere = ROWS + COLS
    top, bottom = r == 0, r == row_last
    west_end, east_end = k == 0, k == col_last
    down = bottom.astype(jnp.int32)
    right = east_end.astype(jnp.int32)
    in_corner = (top | bottom) & (west_end | east_end)
    corners = [(i, j) for i in (0, row_last) for j in (0, col_last)]
    edge_rows = [(i, j) for i in (0, row_last) for j in range(1, col_last)]
    edge_cols = [(i, j) for i in range(1, row_last) for j in (0, col_last)]

    def late(i):
        return i % 2 ^ i // (n_row // 2)

    def swap(x, where, image, late_image=None):
        pairs = []
        for i, j in where:
            to = late_image if late_image and late(i) else image
            other = (row_last - i if to & 2 else i) * n_col + (col_last - j if to & 1 else j)
            pairs.append((i * n_col + j, other))
        return lax.ppermute(x, everywhere, pairs)

    north, south = cells[:, :, :2], cells[:, :, height - 2 :]
    from_above = lax.ppermute(south, ROWS, [(i, i + 1) for i in range(row_last)])
    from_below = lax.ppermute(north, ROWS, [(i + 1, i) for i in range(row_last)])

    def side_columns(above, below, columns):
        return jnp.concatenate([above[:, columns], cells[:, columns], below[:, columns]], axis=2)

    west, east = slice(0, 2), slice(width - 2, width)

    def sideways(above, below, rows):
        steps = [(i * n_col + j, i * n_col + j + 1) for i in rows for j in range(col_last)]
        from_left = lax.ppermute(side_columns(above, below, east), everywhere, steps)
        from_right = lax.ppermute(side_columns(above, below, west), everywhere, [(b, a) for a, b in steps])
        return from_left, from_right

    left_inner, right_inner = sideways(from_above, from_below, range(1, row_last))

    own_row = jnp.where(top, north, jnp.flip(south, 2))

    own_col = jnp.where(
        west_end,
        side_columns(from_above, from_below, west),
        jnp.flip(side_columns(from_above, from_below, east), 1),
    )
    tall = height + 4
    row_image = swap(own_row, edge_rows, 1)
    col_image = swap(own_col, edge_cols, 3, 1)
    both_image = swap(jnp.concatenate([own_col, turned(own_row)], axis=2), corners, 3)
    row_image = jnp.where(in_corner, turned(both_image[:, :, tall:]), row_image)
    col_image = jnp.where(in_corner, both_image[:, :, :tall], col_image)

    def row_seam(is_top):
        code = jnp.where(is_top, seam_code[:, 0], seam_code[:, 1])
        face = jnp.where(is_top, seam_face[:, 0], seam_face[:, 1])
        side = jnp.where(is_top, 0, 1)
        return 2 * ((code >> 1) ^ side) + (code & 1), face

    col_late = ~in_corner & (late(r) == 1)
    col_first = jnp.where(col_late, 1, 3)
    col_next = jnp.where(col_late, 3, 1)
    row_first = jnp.where(in_corner, 3, 1)
    row_next = jnp.where(in_corner, 1, 2)
    row_from, row_face = row_seam(top)
    give_from, give_face = row_seam(jnp.where(in_corner, top, ~top))

    def column_seam(is_west):
        code = jnp.where(is_west, seam_code[:, 2], seam_code[:, 3])
        face = jnp.where(is_west, seam_face[:, 2], seam_face[:, 3])
        at = jnp.where(is_west, 0, 1)
        side = down ^ (code & 1)
        inner = jnp.where(side == 0, looked_up(seam_code[:, 0], face), looked_up(seam_code[:, 1], face))
        inner_face = jnp.where(side == 0, looked_up(seam_face[:, 0], face), looked_up(seam_face[:, 1], face))
        inner_east = (code >> 1) ^ (inner & 1)
        inner_from = 2 * ((inner >> 1) ^ down) + (inner_east ^ at)
        return 2 * (code & 1) + ((code >> 1) ^ at), face, inner_from, inner_face, inner_east

    col_from, col_face, block_from, block_face, block_east = column_seam(west_end)
    give_col, give_col_face, give_block, give_block_face, give_east = column_seam(~west_end)

    def spot(comes_from, first, face):
        return jnp.where(comes_from == first, count, 0) + face

    row_all = chosen(
        jnp.concatenate([own_row, row_image]),
        jnp.concatenate(
            [
                spot(row_from, row_first, row_face),
                spot(give_from ^ row_next, row_first, give_face),
                spot(block_from, 3, block_face),
                spot(give_block ^ 1, 3, give_block_face),
            ]
        ),
    )
    col_all = chosen(
        jnp.concatenate([own_col, col_image]),
        jnp.concatenate([spot(col_from, col_first, col_face), spot(give_col ^ col_next, col_first, give_col_face)]),
    )

    def block(rows, is_east):
        return per_face(is_east == 0, rows[:, west], jnp.flip(rows[:, east], 1))

    row_here, row_gift = row_all[:count], row_all[count : 2 * count]
    block_here = block(row_all[2 * count : 3 * count], block_east)
    col_here = col_all[:count]
    col_gift, block_gift = col_all[count:], block(row_all[3 * count :], give_east)
    row_given = swap(row_gift, edge_rows, 2)
    col_given = swap(col_gift, edge_cols, 1, 3)
    both_given = swap(jnp.concatenate([col_gift, turned(row_gift), block_gift], axis=2), corners, 1)
    row_given = jnp.where(in_corner, turned(both_given[:, :, tall : tall + width]), row_given)
    col_given = jnp.where(in_corner, both_given[:, :, :tall], col_given)
    block_given = both_given[:, :, tall + width :]

    def at_hand(comes_from, first):
        return (comes_from == 0) | (comes_from == first)

    row_pick = per_face(at_hand(row_from, row_first), row_here, row_given)
    row_pick = per_face(row_from & 1 == 1, jnp.flip(row_pick, 1), row_pick)
    above = jnp.where(top, jnp.flip(row_pick, 2), from_above)
    below = jnp.where(bottom, row_pick, from_below)
    left_edge, right_edge = sideways(above, below, (0, row_last))
    from_left = jnp.where(top | bottom, left_edge, left_inner)
    from_right = jnp.where(top | bottom, right_edge, right_inner)

    col_pick = per_face(at_hand(col_from, col_first), col_here, col_given)
    col_pick = per_face(col_from & 2 == 2, jnp.flip(col_pick, 2), col_pick)
    corner = per_face(at_hand(block_from, 3), block_here, block_given)
    mask = jnp.where(
        top,
        jnp.where(west_end, corner_mask[:, 0], corner_mask[:, 1]),
        jnp.where(west_end, corner_mask[:, 2], corner_mask[:, 3]),
    )
    corner = per_face(mask == 0, 0, corner)
    edge = jnp.concatenate(
        [
            jnp.where(top, jnp.flip(corner, 2), col_pick[:, :, :2]),
            col_pick[:, :, 2 : height + 2],
            jnp.where(bottom, corner, col_pick[:, :, height + 2 :]),
        ],
        axis=2,
    )
    left_cols = jnp.where(west_end, jnp.flip(edge, 1), from_left)
    right_cols = jnp.where(east_end, edge, from_right)
    return left_cols, right_cols, above, below


def compute_kernel(
    core_ref,
    st_ref,
    lf_ref,
    rt_ref,
    up_ref,
    lo_ref,
    wg_ref,
    wd_ref,
    hg_ref,
    hidden_ref,
    mine_ref,
    theirs_ref,
    x_ref,
    dg_ref,
    dv_ref,
    sums_ref,
    sems,
):
    _, faces, wide, height, c_in = x_ref.shape
    width = wide - 4
    c_out = hg_ref.shape[-1]
    dg_ref[...] = jnp.zeros(dg_ref.shape, dg_ref.dtype)
    dv_ref[...] = jnp.zeros(dv_ref.shape, dv_ref.dtype)
    step = 1
    cells = step * width * height

    def forward(n, _):
        f = n * step
        here = pl.ds(f, step)

        inside = pl.ds(2, width)
        mid = st_ref[here]
        x_ref[2, here, inside] = mid
        mid = mid.astype(jnp.float32)
        above = up_ref[here].astype(jnp.float32)
        below = lo_ref[here].astype(jnp.float32)
        left = lf_ref[here].astype(jnp.float32)
        right = rt_ref[here].astype(jnp.float32)
        for shift in range(5):
            rows = slice(shift, shift + height)
            x_ref[shift, here, pl.ds(0, 2)] = left[:, :, rows].astype(jnp.bfloat16)
            x_ref[shift, here, pl.ds(width + 2, 2)] = right[:, :, rows].astype(jnp.bfloat16)
        for shift, parts in (
            (0, [above, mid[:, :, : height - 2]]),
            (1, [above[:, :, 1:], mid[:, :, : height - 1]]),
            (3, [mid[:, :, 1:], below[:, :, :1]]),
            (4, [mid[:, :, 2:], below]),
        ):
            x_ref[shift, here, inside] = jnp.concatenate(parts, axis=2).astype(jnp.bfloat16)

        def windows(spacing, first):
            return jnp.concatenate(
                [
                    x_ref[first + a * spacing, here, pl.ds(first + b * spacing, width)].reshape(cells, c_in)
                    for a in range(3)
                    for b in range(3)
                ],
                axis=1,
            )

        gate = jnp.dot(windows(1, 1), wg_ref[...], preferred_element_type=jnp.float32)
        value = jnp.dot(windows(2, 0), wd_ref[...], preferred_element_type=jnp.float32)
        root = (2.0 / jnp.pi) ** 0.5
        square = gate * gate
        t = jnp.tanh(root * gate * (1.0 + 0.044715 * square))
        half = 0.5 * (1.0 + t)
        act = gate * half
        slope = half + 0.5 * gate * (1.0 - t * t) * (root * (1.0 + 3 * 0.044715 * square))
        shape = (step, width, height, c_out)
        up = hg_ref[here].astype(jnp.float32).reshape(cells, c_out)
        hidden_ref[here] = (act * value).astype(jnp.bfloat16).reshape(shape)
        dgate = (up * value * slope).astype(jnp.bfloat16).reshape(shape)
        dvalue = (up * act).astype(jnp.bfloat16).reshape(shape)
        for b in range(3):
            lanes = pl.ds(b * c_out, c_out)
            dg_ref[here, pl.ds(b, width), :, lanes] = dgate
            dv_ref[here, pl.ds(2 * b, width), :, lanes] = dvalue
        return 0

    lax.fori_loop(0, faces // step, forward, 0, unroll=True)

    _, across, _, along, span, _ = sums_ref.shape

    def put(grad, tap, block):
        start, end = tap * c_in, (tap + 1) * c_in
        at = start
        while at < end:
            n = at // span
            stop = min(end, (n + 1) * span)
            spot = n // 2 % across, n // 2 // across
            sums_ref[n % 2, spot[0], grad, spot[1], pl.ds(at - n * span, stop - at)] = block[at - start : stop - start]
            at = stop

    core = core_ref[0]
    copies = []
    for grad, first, cols, delta in ((0, 1, pl.ds(1, wide - 2), dg_ref), (1, 0, pl.ds(0, wide), dv_ref)):
        d = delta[...].reshape(-1, 3 * c_out)
        for a in range(3):
            x = x_ref[first + a * (grad + 1), :, cols].reshape(-1, c_in)
            sums = lax.dot_general(x, d, (((0,), (0,)), ((), ())), preferred_element_type=jnp.float32)
            for b in range(3):
                put(grad, a * 3 + b, sums[:, b * c_out : (b + 1) * c_out])
        for n, target in ((core, mine_ref), (1 - core, theirs_ref)):
            copy = pltpu.make_async_copy(sums_ref.at[n, :, grad], target.at[:, grad], sems.at[len(copies)])
            copy.start()
            copies.append(copy)
    for copy in copies:
        copy.wait()


def compute(core, st, lf, rt, up, lo, wg, wd, hg):
    faces, width, height, c_in = st.shape
    wide = width + 4
    c_out = wg.shape[-1]
    across, along = lax.axis_size("x"), lax.axis_size("yh")
    shares = (across, 2, along, 9 * c_in // (2 * across * along), c_out)
    vm = pl.BlockSpec(memory_space=pltpu.VMEM)
    anywhere = pl.BlockSpec(memory_space=pl.ANY)
    return pl.pallas_call(
        compute_kernel,
        in_specs=[pl.BlockSpec(memory_space=pltpu.SMEM)] + [vm] * 8,
        out_specs=[vm, anywhere, anywhere],
        out_shape=[
            jax.ShapeDtypeStruct(hg.shape, jnp.bfloat16),
            jax.ShapeDtypeStruct(shares, jnp.float32),
            jax.ShapeDtypeStruct(shares, jnp.float32),
        ],
        scratch_shapes=[
            pltpu.VMEM((5, faces, wide, height, c_in), jnp.bfloat16),
            pltpu.VMEM((faces, wide - 2, height, 3 * c_out), jnp.bfloat16),
            pltpu.VMEM((faces, wide, height, 3 * c_out), jnp.bfloat16),
            pltpu.VMEM((2,) + shares, jnp.float32),
            pltpu.SemaphoreType.DMA((4,)),
        ],
        compiler_params=pltpu.CompilerParams(vmem_limit_bytes=56 * 2**20),
        name="gated_conv",
    )(core, st, lf, rt, up, lo, wg.reshape(-1, c_out), wd.reshape(-1, c_out), hg)


def on_device(state, gate_kernel, dilated_kernel, hidden_grad, seam_face, seam_code, corner_mask):
    count, height, width, _ = state.shape
    cells = turned(state)
    left, right, above, below = halos(cells, seam_face, seam_code, corner_mask)
    core = lax.axis_index("c").reshape(1)
    hidden, mine, theirs = compute(
        core, cells, left, right, above, below, gate_kernel, dilated_kernel, turned(hidden_grad)
    )
    total_cells = count * height * width * lax.axis_size(ROWS) * lax.axis_size(COLS)
    gate_part, dilated_part = scattered_sum(mine, theirs, total_cells ** (-0.5))
    return (turned(hidden), gate_part, dilated_part)


def scattered_sum(mine, theirs, scale):
    both = mine + lax.ppermute(theirs, "c", [(0, 1), (1, 0)])
    across, grads, along, span, lanes = both.shape
    arrived = lax.all_to_all(both.astype(jnp.bfloat16).reshape(across, -1, lanes), "x", 0, 0)
    part = jnp.sum(arrived.astype(jnp.float32), axis=0).reshape(grads, along, span, lanes)
    takers = lax.axis_size(COLS)
    share = span * lanes // takers
    tall = -(-(share + lanes // 2) // lanes)
    starts = [i * share // lanes for i in range(takers)]
    part = part.astype(jnp.bfloat16)
    sends = jnp.stack([part[:, :, s : s + tall] for s in starts])
    sends = jnp.transpose(sends, (2, 0, 3, 1, 4)).reshape(along * takers, tall, grads, lanes)
    arrived = lax.all_to_all(sends, ("yh",) + COLS, 0, 0)
    total = jnp.transpose(jnp.sum(arrived.astype(jnp.float32), axis=0) * scale, (1, 0, 2)).reshape(grads, tall * lanes)
    skip = lax.axis_index(COLS) * share % lanes
    total = lax.dynamic_slice_in_dim(total, skip, share, axis=1)
    return total[0], total[1]


def solution(mesh):
    fine = Mesh(mesh.devices.reshape(2, 4, 2, 4, 8), ROWS + COLS)
    cells = P(None, ROWS, COLS, None)
    return jax.shard_map(
        on_device,
        mesh=fine,
        in_specs=(cells, P(), P(), cells, P(), P(), P()),
        out_specs=(cells, P(ROWS + COLS), P(ROWS + COLS)),
        check_vma=False,
    )
```

```python
import jax
import jax.numpy as jnp
from jax import lax
from jax.experimental import pallas as pl
from jax.experimental.pallas import tpu as pltpu
from jax.sharding import Mesh
from jax.sharding import PartitionSpec as P

ROWS = ("yh", "x", "c")
COLS = ("yl", "z")


def turned(cells):
    return jnp.transpose(cells, (0, 2, 1, 3))


def chosen(table, index):
    return table.at[index].get(mode="promise_in_bounds")


def looked_up(table, index):
    spots = jnp.arange(table.shape[0])
    return jnp.sum(jnp.where(index[:, None] == spots[None, :], table[None, :], 0), axis=1)


def per_face(condition, yes, no):
    return jnp.where(condition[:, None, None, None], yes, no)


def halos(cells, seam_face, seam_code, corner_mask):
    count, width, height, _ = cells.shape
    n_row = lax.axis_size(ROWS)
    n_col = lax.axis_size(COLS)
    r = lax.axis_index(ROWS)
    k = lax.axis_index(COLS)
    row_last = n_row - 1
    col_last = n_col - 1
    everywhere = ROWS + COLS
    top, bottom = r == 0, r == row_last
    west_end, east_end = k == 0, k == col_last
    down = bottom.astype(jnp.int32)
    right = east_end.astype(jnp.int32)
    in_corner = (top | bottom) & (west_end | east_end)
    corners = [(i, j) for i in (0, row_last) for j in (0, col_last)]
    edge_rows = [(i, j) for i in (0, row_last) for j in range(1, col_last)]
    edge_cols = [(i, j) for i in range(1, row_last) for j in (0, col_last)]

    def late(i):
        return i % 2 ^ i // (n_row // 2)

    def swap(x, where, image, late_image=None):
        pairs = []
        for i, j in where:
            to = late_image if late_image and late(i) else image
            other = (row_last - i if to & 2 else i) * n_col + (col_last - j if to & 1 else j)
            pairs.append((i * n_col + j, other))
        return lax.ppermute(x, everywhere, pairs)

    north, south = cells[:, :, :2], cells[:, :, height - 2 :]
    from_above = lax.ppermute(south, ROWS, [(i, i + 1) for i in range(row_last)])
    from_below = lax.ppermute(north, ROWS, [(i + 1, i) for i in range(row_last)])

    def side_columns(above, below, columns):
        return jnp.concatenate([above[:, columns], cells[:, columns], below[:, columns]], axis=2)

    west, east = slice(0, 2), slice(width - 2, width)

    def sideways(above, below, rows):
        steps = [(i * n_col + j, i * n_col + j + 1) for i in rows for j in range(col_last)]
        from_left = lax.ppermute(side_columns(above, below, east), everywhere, steps)
        from_right = lax.ppermute(side_columns(above, below, west), everywhere, [(b, a) for a, b in steps])
        return from_left, from_right

    left_inner, right_inner = sideways(from_above, from_below, range(1, row_last))

    own_row = jnp.where(top, north, jnp.flip(south, 2))

    own_col = jnp.where(
        west_end,
        side_columns(from_above, from_below, west),
        jnp.flip(side_columns(from_above, from_below, east), 1),
    )
    tall = height + 4
    row_image = swap(own_row, edge_rows, 1)
    col_image = swap(own_col, edge_cols, 3, 1)
    both_image = swap(jnp.concatenate([own_col, turned(own_row)], axis=2), corners, 3)
    row_image = jnp.where(in_corner, turned(both_image[:, :, tall:]), row_image)
    col_image = jnp.where(in_corner, both_image[:, :, :tall], col_image)

    def row_seam(is_top):
        code = jnp.where(is_top, seam_code[:, 0], seam_code[:, 1])
        face = jnp.where(is_top, seam_face[:, 0], seam_face[:, 1])
        side = jnp.where(is_top, 0, 1)
        return 2 * ((code >> 1) ^ side) + (code & 1), face

    col_late = ~in_corner & (late(r) == 1)
    col_first = jnp.where(col_late, 1, 3)
    col_next = jnp.where(col_late, 3, 1)
    row_first = jnp.where(in_corner, 3, 1)
    row_next = jnp.where(in_corner, 1, 2)
    row_from, row_face = row_seam(top)
    give_from, give_face = row_seam(jnp.where(in_corner, top, ~top))

    def column_seam(is_west):
        code = jnp.where(is_west, seam_code[:, 2], seam_code[:, 3])
        face = jnp.where(is_west, seam_face[:, 2], seam_face[:, 3])
        at = jnp.where(is_west, 0, 1)
        side = down ^ (code & 1)
        inner = jnp.where(side == 0, looked_up(seam_code[:, 0], face), looked_up(seam_code[:, 1], face))
        inner_face = jnp.where(side == 0, looked_up(seam_face[:, 0], face), looked_up(seam_face[:, 1], face))
        inner_east = (code >> 1) ^ (inner & 1)
        inner_from = 2 * ((inner >> 1) ^ down) + (inner_east ^ at)
        return 2 * (code & 1) + ((code >> 1) ^ at), face, inner_from, inner_face, inner_east

    col_from, col_face, block_from, block_face, block_east = column_seam(west_end)
    give_col, give_col_face, give_block, give_block_face, give_east = column_seam(~west_end)

    def spot(comes_from, first, face):
        return jnp.where(comes_from == first, count, 0) + face

    row_all = chosen(
        jnp.concatenate([own_row, row_image]),
        jnp.concatenate(
            [
                spot(row_from, row_first, row_face),
                spot(give_from ^ row_next, row_first, give_face),
                spot(block_from, 3, block_face),
                spot(give_block ^ 1, 3, give_block_face),
            ]
        ),
    )
    col_all = chosen(
        jnp.concatenate([own_col, col_image]),
        jnp.concatenate([spot(col_from, col_first, col_face), spot(give_col ^ col_next, col_first, give_col_face)]),
    )

    def block(rows, is_east):
        return per_face(is_east == 0, rows[:, west], jnp.flip(rows[:, east], 1))

    row_here, row_gift = row_all[:count], row_all[count : 2 * count]
    block_here = block(row_all[2 * count : 3 * count], block_east)
    col_here = col_all[:count]
    col_gift, block_gift = col_all[count:], block(row_all[3 * count :], give_east)
    row_given = swap(row_gift, edge_rows, 2)
    col_given = swap(col_gift, edge_cols, 1, 3)
    both_given = swap(jnp.concatenate([col_gift, turned(row_gift), block_gift], axis=2), corners, 1)
    row_given = jnp.where(in_corner, turned(both_given[:, :, tall : tall + width]), row_given)
    col_given = jnp.where(in_corner, both_given[:, :, :tall], col_given)
    block_given = both_given[:, :, tall + width :]

    def at_hand(comes_from, first):
        return (comes_from == 0) | (comes_from == first)

    row_pick = per_face(at_hand(row_from, row_first), row_here, row_given)
    row_pick = per_face(row_from & 1 == 1, jnp.flip(row_pick, 1), row_pick)
    above = jnp.where(top, jnp.flip(row_pick, 2), from_above)
    below = jnp.where(bottom, row_pick, from_below)
    left_edge, right_edge = sideways(above, below, (0, row_last))
    from_left = jnp.where(top | bottom, left_edge, left_inner)
    from_right = jnp.where(top | bottom, right_edge, right_inner)

    col_pick = per_face(at_hand(col_from, col_first), col_here, col_given)
    col_pick = per_face(col_from & 2 == 2, jnp.flip(col_pick, 2), col_pick)
    corner = per_face(at_hand(block_from, 3), block_here, block_given)
    mask = jnp.where(
        top,
        jnp.where(west_end, corner_mask[:, 0], corner_mask[:, 1]),
        jnp.where(west_end, corner_mask[:, 2], corner_mask[:, 3]),
    )
    corner = per_face(mask == 0, 0, corner)
    edge = jnp.concatenate(
        [
            jnp.where(top, jnp.flip(corner, 2), col_pick[:, :, :2]),
            col_pick[:, :, 2 : height + 2],
            jnp.where(bottom, corner, col_pick[:, :, height + 2 :]),
        ],
        axis=2,
    )
    left_cols = jnp.where(west_end, jnp.flip(edge, 1), from_left)
    right_cols = jnp.where(east_end, edge, from_right)
    return left_cols, right_cols, above, below


def compute_kernel(
    core_ref,
    st_ref,
    lf_ref,
    rt_ref,
    up_ref,
    lo_ref,
    wg_ref,
    wd_ref,
    hg_ref,
    hidden_ref,
    mine_ref,
    theirs_ref,
    x_ref,
    d_ref,
    sums_ref,
    sems,
):
    _, faces, wide, height, c_in = x_ref.shape
    width = wide - 4
    c_out = hg_ref.shape[-1]
    step = 1
    cells = step * width * height

    def forward(n, _):
        f = n * step
        here = pl.ds(f, step)

        inside = pl.ds(2, width)
        mid = st_ref[here]
        x_ref[2, here, inside] = mid
        mid = mid.astype(jnp.float32)
        above = up_ref[here].astype(jnp.float32)
        below = lo_ref[here].astype(jnp.float32)
        left = lf_ref[here].astype(jnp.float32)
        right = rt_ref[here].astype(jnp.float32)
        for shift in range(5):
            rows = slice(shift, shift + height)
            x_ref[shift, here, pl.ds(0, 2)] = left[:, :, rows].astype(jnp.bfloat16)
            x_ref[shift, here, pl.ds(width + 2, 2)] = right[:, :, rows].astype(jnp.bfloat16)
        for shift, parts in (
            (0, [above, mid[:, :, : height - 2]]),
            (1, [above[:, :, 1:], mid[:, :, : height - 1]]),
            (3, [mid[:, :, 1:], below[:, :, :1]]),
            (4, [mid[:, :, 2:], below]),
        ):
            x_ref[shift, here, inside] = jnp.concatenate(parts, axis=2).astype(jnp.bfloat16)

        def windows(spacing, first):
            return jnp.concatenate(
                [
                    x_ref[first + a * spacing, here, pl.ds(first + b * spacing, width)].reshape(cells, c_in)
                    for a in range(3)
                    for b in range(3)
                ],
                axis=1,
            )

        gate = jnp.dot(windows(1, 1), wg_ref[...], preferred_element_type=jnp.float32)
        value = jnp.dot(windows(2, 0), wd_ref[...], preferred_element_type=jnp.float32)
        root = (2.0 / jnp.pi) ** 0.5
        square = gate * gate
        t = jnp.tanh(root * gate * (1.0 + 0.044715 * square))
        half = 0.5 * (1.0 + t)
        act = gate * half
        slope = half + 0.5 * gate * (1.0 - t * t) * (root * (1.0 + 3 * 0.044715 * square))
        shape = (step, width, height, c_out)
        up = hg_ref[here].astype(jnp.float32).reshape(cells, c_out)
        hidden_ref[here] = (act * value).astype(jnp.bfloat16).reshape(shape)
        dgate = (up * value * slope).astype(jnp.bfloat16).reshape(shape)
        dvalue = (up * act).astype(jnp.bfloat16).reshape(shape)
        for tap, (at, delta) in enumerate([(1 + b, dgate) for b in range(3)] + [(2 * b, dvalue) for b in range(3)]):
            lanes = pl.ds(tap * c_out, c_out)
            for start, size in ((0, at), (at + width, 4 - at)):
                if size > 0:
                    blank = jnp.zeros((step, size, height, c_out), jnp.bfloat16)
                    d_ref[here, pl.ds(start, size), :, lanes] = blank
            d_ref[here, pl.ds(at, width), :, lanes] = delta
        return 0

    lax.fori_loop(0, faces // step, forward, 0, unroll=True)

    _, across, _, along, span, _ = sums_ref.shape

    def put(grad, tap, block):
        start, end = tap * c_in, (tap + 1) * c_in
        at = start
        while at < end:
            n = at // span
            stop = min(end, (n + 1) * span)
            spot = n // 2 % across, n // 2 // across
            sums_ref[n % 2, spot[0], grad, spot[1], pl.ds(at - n * span, stop - at)] = block[at - start : stop - start]
            at = stop

    core = core_ref[0]
    copies = []
    half = 3 * c_out
    everything, inner = pl.ds(0, wide), pl.ds(1, wide - 2)
    for grad, parts in (
        (1, ((0, everything, half, half), (4, everything, half, half), (2, everything, 0, 2 * half))),
        (0, ((1, inner, 0, half), (3, inner, 0, half))),
    ):
        for shift, cols, lane, lanes in parts:
            x = x_ref[shift, :, cols].reshape(-1, c_in)
            d = d_ref[:, cols, :, pl.ds(lane, lanes)].reshape(-1, lanes)
            sums = lax.dot_general(x, d, (((0,), (0,)), ((), ())), preferred_element_type=jnp.float32)
            for b in range(lanes // c_out):
                which, tap = divmod(lane // c_out + b, 3)
                a = shift // 2 if which == 1 else shift - 1
                put(which, a * 3 + tap, sums[:, b * c_out : (b + 1) * c_out])
        for n, target in ((core, mine_ref), (1 - core, theirs_ref)):
            copy = pltpu.make_async_copy(sums_ref.at[n, :, grad], target.at[:, grad], sems.at[len(copies)])
            copy.start()
            copies.append(copy)
    for copy in copies:
        copy.wait()


def compute(core, st, lf, rt, up, lo, wg, wd, hg):
    faces, width, height, c_in = st.shape
    wide = width + 4
    c_out = wg.shape[-1]
    across, along = lax.axis_size("x"), lax.axis_size("yh")
    shares = (across, 2, along, 9 * c_in // (2 * across * along), c_out)
    vm = pl.BlockSpec(memory_space=pltpu.VMEM)
    anywhere = pl.BlockSpec(memory_space=pl.ANY)
    return pl.pallas_call(
        compute_kernel,
        in_specs=[pl.BlockSpec(memory_space=pltpu.SMEM)] + [vm] * 8,
        out_specs=[vm, anywhere, anywhere],
        out_shape=[
            jax.ShapeDtypeStruct(hg.shape, jnp.bfloat16),
            jax.ShapeDtypeStruct(shares, jnp.float32),
            jax.ShapeDtypeStruct(shares, jnp.float32),
        ],
        scratch_shapes=[
            pltpu.VMEM((5, faces, wide, height, c_in), jnp.bfloat16),
            pltpu.VMEM((faces, wide, height, 6 * c_out), jnp.bfloat16),
            pltpu.VMEM((2,) + shares, jnp.float32),
            pltpu.SemaphoreType.DMA((4,)),
        ],
        compiler_params=pltpu.CompilerParams(vmem_limit_bytes=56 * 2**20),
        name="gated_conv",
    )(core, st, lf, rt, up, lo, wg.reshape(-1, c_out), wd.reshape(-1, c_out), hg)


def on_device(state, gate_kernel, dilated_kernel, hidden_grad, seam_face, seam_code, corner_mask):
    count, height, width, _ = state.shape
    cells = turned(state)
    left, right, above, below = halos(cells, seam_face, seam_code, corner_mask)
    core = lax.axis_index("c").reshape(1)
    hidden, mine, theirs = compute(
        core, cells, left, right, above, below, gate_kernel, dilated_kernel, turned(hidden_grad)
    )
    total_cells = count * height * width * lax.axis_size(ROWS) * lax.axis_size(COLS)
    gate_part, dilated_part = scattered_sum(mine, theirs, total_cells ** (-0.5))
    return (turned(hidden), gate_part, dilated_part)


def scattered_sum(mine, theirs, scale):
    both = mine + lax.ppermute(theirs, "c", [(0, 1), (1, 0)])
    across, grads, along, span, lanes = both.shape
    arrived = lax.all_to_all(both.astype(jnp.bfloat16).reshape(across, -1, lanes), "x", 0, 0)
    part = jnp.sum(arrived.astype(jnp.float32), axis=0).reshape(grads, along, span, lanes)
    takers = lax.axis_size(COLS)
    share = span * lanes // takers
    tall = -(-(share + lanes // 2) // lanes)
    starts = [i * share // lanes for i in range(takers)]
    part = part.astype(jnp.bfloat16)
    sends = jnp.stack([part[:, :, s : s + tall] for s in starts])
    sends = jnp.transpose(sends, (2, 0, 3, 1, 4)).reshape(along * takers, tall, grads, lanes)
    arrived = lax.all_to_all(sends, ("yh",) + COLS, 0, 0)
    total = jnp.transpose(jnp.sum(arrived.astype(jnp.float32), axis=0) * scale, (1, 0, 2)).reshape(grads, tall * lanes)
    skip = lax.axis_index(COLS) * share % lanes
    total = lax.dynamic_slice_in_dim(total, skip, share, axis=1)
    return total[0], total[1]


def solution(mesh):
    fine = Mesh(mesh.devices.reshape(2, 4, 2, 4, 8), ROWS + COLS)
    cells = P(None, ROWS, COLS, None)
    return jax.shard_map(
        on_device,
        mesh=fine,
        in_specs=(cells, P(), P(), cells, P(), P(), P()),
        out_specs=(cells, P(ROWS + COLS), P(ROWS + COLS)),
        check_vma=False,
    )
```
